256 devices in a mesh: role: 2 (over z_hi), expert: 32 (over y, x, core), tensor: 4 (over z_lo).
Axes of the slice: x: 4, y: 4, z: 8 (z_hi: 2, z_lo: 4; z = z_hi * 4 + z_lo), core: 2. Of those that a mesh axis runs over, the one named last changes fastest.
Arguments:
- request_latent_cache: bfloat16 [128, 4096, 576], P(('role', 'expert'), 'tensor'), may hold values from -6 to 6
- queries: bfloat16 [128, 128, 576], P(('role', 'expert')), may hold values from -32 to 32
- cache_lengths: int32 [128], P(('role', 'expert')), may hold values from 1024 to 4096, as said below
- residual_in: bfloat16 [128, 7168], P(('role', 'expert')), may hold values from -4 to 4
- value_up_weight: bfloat16 [128, 512, 128], P(('expert', 'tensor')), may hold values from -2 to 2
- out_proj: bfloat16 [16384, 7168], P(('expert', 'tensor')), may hold values from -0.046875 to 0.046875
- norm_gain: bfloat16 [7168], replicated, may hold values from 0.25 to 1.75
- gate_proj: bfloat16 [32, 7168, 1024], P('expert', None, ('role', 'tensor')), may hold values from -0.0625 to 0.0625
- up_proj: bfloat16 [32, 7168, 1024], P('expert', None, ('role', 'tensor')), may hold values from -0.0625 to 0.0625
- down_proj: bfloat16 [32, 1024, 7168], P('expert', ('role', 'tensor')), may hold values from -0.1875 to 0.1875
- expert_ids: int32 [128, 8], P(('role', 'expert')), may hold values from 0 to 31, all different within a row; in each aligned block of 128 rows (0 to 127, 128 to 255, ...) at most 64 rows name the same one
- route_weights: bfloat16 [128, 8], P(('role', 'expert')), may hold values from 0.099609375 to 0.59765625
Outputs:
- attended: float32 [128, 7168], P(('role', 'expert'))
- routed: float32 [128, 7168], P(('role', 'expert'))
The draws below stay inside these ranges and needn't reach their ends.
Inputs may be any that keep to these rules, and one draw needn't show every extreme that they name: `cache_lengths`: slots below a request's length are live; some request uses all 4096. `expert_ids`: each token names 8 different experts; no expert is named by more than 64 tokens, a bound that some block reaches.
All inputs are finite; a program needn't handle non-finite values.
Results may differ from the reference program's by a relative error of at most 0.013.
Values may be sent and summed in bfloat16 or wider, within the bound.
No kernel may reach another device: no remote copies, remote signals or barrier semaphores. Data moves between devices by JAX's collectives and lax.ppermute only.
A program may use at most 64 MiB of HBM per device.

```python
import math
import jax
import jax.numpy as jnp
import numpy as np
from jax import lax

D = 7168
HEADS = 128
KV_RANK = 512
ROPE = 64
HEAD_V = 128
FF = 1024
TOP = 8
CACHE_LEN = 4096
EXPERTS = 32
REQUESTS = 128
CAPACITY = 64


def base_cache(key):
    return jnp.clip(jax.random.normal(key, (REQUESTS, CACHE_LEN, KV_RANK + ROPE), jnp.float32), -6.0, 6.0)


def draw_request_latent_cache(key, part):
    values = base_cache(key)
    return values.astype(jnp.bfloat16)


def draw_queries(key, part):
    key = jax.random.fold_in(key, 23)
    values = jnp.clip(jax.random.normal(key, (REQUESTS, HEADS, KV_RANK + ROPE), jnp.float32), -6.0, 6.0)
    return values.astype(jnp.bfloat16)


def draw_cache_lengths(key, part):
    key = jax.random.fold_in(key, 37)
    values = jax.random.randint(key, (REQUESTS,), CACHE_LEN // 4, CACHE_LEN + 1, dtype=jnp.int32)
    return values.at[0].set(CACHE_LEN)


def level_of(key, dims, shards, least, largest):
    level, own = 1.0, jax.random.fold_in(key, 6)
    for axis_at, parts in shards:
        steps = jnp.exp(jax.random.uniform(jax.random.fold_in(own, axis_at), (parts,), jnp.float32, least / len(shards), largest / len(shards)))
        level = level * jnp.repeat(steps, dims[axis_at] // parts).reshape([-1 if axis == axis_at else 1 for axis in range(len(dims))])
    return level


def assign_block(key, own, number, rows, count, top, limit, skew):
    sequence = jax.random.permutation(key, count)
    crowded, ordinary = load_shares(count, rows * top, limit, skew, True), load_shares(count, rows * top, limit, skew, False)
    places = jnp.arange(count)

    def named(lengths, rotation):
        used = int((lengths > 0).sum())
        fixed = max(1, used // 4)
        passed = fixed + (places - fixed + rotation * (used - fixed)) % max(1, count - fixed)
        return jnp.zeros((count,), jnp.int32).at[sequence[jnp.where(places < fixed, places, passed)]].set(jnp.asarray(lengths, jnp.int32))

    lengths = jnp.where(number % 4 == 0, named(crowded, number // 4), named(ordinary, number - number // 4 - 1))
    mixed = jax.random.permutation(jax.random.fold_in(own, 3), count)
    donor, sink = mixed[0:count // 2 * 2:2], mixed[1:count // 2 * 2:2]
    margin = jnp.minimum(lengths[donor] - 1, limit - lengths[sink]) // 2
    margin = jnp.where((donor == sequence[0]) | (sink == sequence[0]) | (lengths[sink] == 0), 0, jnp.maximum(margin, 0))
    passed = jax.random.randint(jax.random.fold_in(own, 4), (count // 2,), 0, 1 << 20) % (margin + 1)
    lengths = lengths.at[donor].add(-passed).at[sink].add(passed)
    labels = jnp.searchsorted(jnp.cumsum(lengths), jnp.arange(rows * top), side="right").astype(jnp.int32)
    grid = labels.reshape(top, rows).T
    grid = grid[jax.random.permutation(jax.random.fold_in(own, 1), rows)]
    rotation = jax.random.randint(jax.random.fold_in(own, 2), (rows, 1), 0, top)
    return jnp.take_along_axis(grid, (jnp.arange(top)[None, :] + rotation) % top, axis=1)


def load_shares(amount, total, reach, skew, full):
    loads = [(1 << 20) // math.isqrt(rank ** skew) + 1 for rank in range(1, amount + 1)]
    largest = reach if full else min(reach, max(-(-total // amount), total * loads[0] // sum(loads)))
    least = 1 if total - largest >= amount - 1 else 0
    given, rest = [largest] + [least] * (amount - 1), total - largest - least * (amount - 1)
    while rest > 0:
        candidates = [i for i in range(1, amount) if given[i] < largest] or [i for i in range(1, amount) if given[i] < reach]
        whole, left = sum([loads[i] for i in candidates]), rest
        for i in candidates:
            addition = min(reach - given[i], max(1, left * loads[i] // whole), rest)
            given[i] = given[i] + addition
            rest = rest - addition
    return np.array(given)


def bell_draw(rng, extent, width, reach, cuts=(), kind=jnp.bfloat16):
    values = width * jax.random.normal(rng, extent, jnp.float32)
    if cuts:
        values = values * level_of(rng, extent, cuts, -0.22, 0.18)
    return jnp.clip(values, -reach, reach).astype(kind)


def setup_inputs(seed: int = 0) -> dict:
    seeds = jax.random.split(jax.random.key(seed), 13)
    request_latent_cache = draw_request_latent_cache(jax.random.fold_in(seeds[12], 71), 0)
    queries = draw_queries(jax.random.fold_in(seeds[12], 71), 0)
    cache_lengths = draw_cache_lengths(jax.random.fold_in(seeds[12], 71), 0)
    residual_in = bell_draw(seeds[3], (REQUESTS, D), 0.5, 4.0, ((0, 64),))
    value_up_weight = bell_draw(seeds[4], (HEADS, KV_RANK, HEAD_V), (max(1, KV_RANK // 64)) ** -0.5, 2.0, ((0, 128),))
    out_proj = bell_draw(seeds[5], (HEADS * HEAD_V, D), (HEADS * HEAD_V) ** -0.5, 0.046875, ((0, 128),))
    norm_gain = jnp.clip(1.0 + 0.15 * jax.random.normal(seeds[6], (D,), jnp.float32), 0.25, 1.75).astype(jnp.bfloat16)
    gate_proj = bell_draw(seeds[7], (EXPERTS, D, FF), D ** -0.5, 0.0625, ((0, 32), (2, 8)))
    up_proj = bell_draw(seeds[8], (EXPERTS, D, FF), D ** -0.5, 0.0625, ((0, 32), (2, 8)))
    down_proj = bell_draw(seeds[9], (EXPERTS, FF, D), FF ** -0.5, 0.1875, ((0, 32), (1, 8)))
    expert_ids_keys = jax.random.split(jax.random.fold_in(seeds[10], 1), REQUESTS // REQUESTS)
    expert_ids_turns = jax.random.permutation(jax.random.fold_in(seeds[10], 3), REQUESTS // REQUESTS)
    expert_ids = jax.vmap(lambda own, number: assign_block(jax.random.fold_in(seeds[10], 2), own, number, REQUESTS, EXPERTS, TOP, CAPACITY, 2))(expert_ids_keys, expert_ids_turns).reshape((REQUESTS, TOP))
    route_weights = jnp.clip(0.099609375 + 0.49804688 * jax.random.uniform(seeds[11], (REQUESTS, TOP), jnp.float32) ** level_of(seeds[11], (REQUESTS, TOP), ((0, 64),), -0.2, 0.2), 0.099609375, 0.59765625).astype(jnp.bfloat16)
    return {"request_latent_cache": request_latent_cache, "queries": queries, "cache_lengths": cache_lengths, "residual_in": residual_in, "value_up_weight": value_up_weight, "out_proj": out_proj, "norm_gain": norm_gain, "gate_proj": gate_proj, "up_proj": up_proj, "down_proj": down_proj, "expert_ids": expert_ids, "route_weights": route_weights}


SCORE_SCALE = 192.0 ** (-0.5)

def attend_one(inputs):
    keys, query, length = inputs
    attention_logits = jnp.dot(query, keys.T, preferred_element_type=jnp.float32) * SCORE_SCALE
    live = (jnp.arange(keys.shape[0], dtype=jnp.int32) < length)[None, :]
    masked = jnp.where(live, attention_logits, -1e+30)
    top = lax.optimization_barrier(jnp.max(masked, axis=1, keepdims=True))
    expo = jnp.where(live, jnp.exp(masked - top), 0.0)
    total = lax.optimization_barrier(jnp.sum(expo, axis=1, keepdims=True))
    numer = jnp.dot(expo.astype(jnp.bfloat16), keys[:, :KV_RANK], preferred_element_type=jnp.float32)
    return (numer / total).astype(jnp.bfloat16)

def reference(request_latent_cache, queries, cache_lengths, residual_in, value_up_weight, out_proj, norm_gain, gate_proj, up_proj, down_proj, expert_ids, route_weights):
    latent_context = lax.map(attend_one, (request_latent_cache, queries, cache_lengths))
    head_output_rows = jnp.einsum('mpq,pqg->mpg', latent_context.astype(jnp.float32), value_up_weight.astype(jnp.float32)).astype(jnp.bfloat16)
    flat = head_output_rows.reshape(head_output_rows.shape[0], -1)
    attn = jnp.dot(flat, out_proj, preferred_element_type=jnp.float32)
    attended = attn + residual_in.astype(jnp.float32)
    mean_square = lax.optimization_barrier(jnp.mean(attended * attended, axis=1, keepdims=True))
    normed = (attended * lax.rsqrt(mean_square + 1e-06) * norm_gain.astype(jnp.float32)).astype(jnp.bfloat16)
    weights = route_weights.astype(jnp.float32)

    def one_expert(running, inputs):
        gate_w, up_w, down_w, which = inputs
        coef = lax.optimization_barrier(jnp.sum(jnp.where(expert_ids == which, weights, 0.0), axis=1))
        gate = jnp.dot(normed, gate_w, preferred_element_type=jnp.float32)
        upper = jnp.dot(normed, up_w, preferred_element_type=jnp.float32)
        act = (jax.nn.silu(gate) * upper).astype(jnp.bfloat16)
        return (running + coef[:, None] * jnp.dot(act, down_w, preferred_element_type=jnp.float32), None)
    start = jnp.zeros((normed.shape[0], normed.shape[1]), jnp.float32)
    routed, _ = lax.scan(one_expert, start, (gate_proj, up_proj, down_proj, jnp.arange(EXPERTS, dtype=jnp.int32)))
    return (attended, routed)
```

```python
import jax
import jax.numpy as jnp
from jax import lax
from jax.sharding import PartitionSpec as P

SCORE_SCALE = 192.0 ** (-0.5)
SIDE = 4
BF = jnp.bfloat16
F32 = jnp.float32


def plane(value, down=0, right=0, core=0):
    pairs = []
    for y in range(SIDE):
        for x in range(SIDE):
            for c in range(2):
                there = ((y + down) % SIDE) * 2 * SIDE + ((x + right) % SIDE) * 2 + (c ^ core)
                pairs.append((y * 2 * SIDE + x * 2 + c, there))
    return lax.ppermute(value, "expert", pairs)


def along(value, step):
    return lax.ppermute(value, "tensor", [(i, (i + step) % 4) for i in range(4)])


def swap(value, bit):
    return lax.ppermute(value, "tensor", [(i, i ^ bit) for i in range(4)])


def other_role(value):
    return lax.ppermute(value, "role", [(0, 1), (1, 0)])


def scatter_sum(acc, **_):
    for axis in ("down", "right"):
        n = acc.shape[0] // SIDE
        sent = acc.astype(BF)
        got = [plane(sent[s * n : (s + 1) * n], **{axis: s}) for s in (2, 1, 3)]
        acc = acc[:n]
        for g in got:
            acc = acc + g.astype(F32)
    return acc


def tensor_sum(value):
    value = value + swap(value, 1)
    return value + swap(value, 2)


def shards(
    request_latent_cache,
    queries,
    cache_lengths,
    residual_in,
    value_up_weight,
    out_proj,
    norm_gain,
    gate_proj,
    up_proj,
    down_proj,
    expert_ids,
    route_weights,
):
    t = lax.axis_index("tensor")
    e = lax.axis_index("expert")
    y, x, c = e // (2 * SIDE), (e // 2) % SIDE, e % 2
    local_requests, local_slots, _ = request_latent_cache.shape
    latent = value_up_weight.shape[1]
    experts = 32

    q = queries.reshape(local_requests, experts, 4, -1)
    q = jnp.take(q, (t + jnp.arange(4)) % 4, axis=2)
    q = jnp.swapaxes(q, 1, 2).reshape(local_requests, 4 * experts, -1)
    logits = (
        jnp.einsum("rhc,rsc->rhs", q, request_latent_cache, preferred_element_type=F32)
        * SCORE_SCALE
    )
    position = t * local_slots + jnp.arange(local_slots, dtype=jnp.int32)
    live = (position[None, :] < cache_lengths[:, None])[:, None, :]
    masked = jnp.where(live, logits, -1e30)
    top = jnp.max(masked, axis=2)
    expo = jnp.where(live, jnp.exp(masked - top[:, :, None]), 0.0)
    total = jnp.sum(expo, axis=2)
    numer = jnp.einsum(
        "rhs,rsc->rhc",
        expo.astype(BF),
        request_latent_cache[:, :, :latent],
        preferred_element_type=F32,
    )
    part = (numer / jnp.maximum(total, 1.0)[:, :, None]).astype(BF)
    part = part.reshape(local_requests, 4, experts, latent)
    stats = jnp.stack([top, total]).reshape(2, local_requests, 4, experts)
    stats_of = [stats[:, :, 0]] + [along(stats[:, :, s], s) for s in (1, 2, 3)]
    parts = [part[:, 0]] + [along(part[:, s], s) for s in (1, 2, 3)]
    tops = jnp.maximum(
        jnp.maximum(stats_of[0][0], stats_of[1][0]), jnp.maximum(stats_of[2][0], stats_of[3][0])
    )
    weights = [jnp.exp(s[0] - tops) * s[1] for s in stats_of]
    whole = weights[0] + weights[1] + weights[2] + weights[3]
    context = sum(
        (w / whole)[:, :, None] * p.astype(F32) for w, p in zip(weights, parts)
    ).astype(BF)
    context = jnp.swapaxes(context, 0, 1)
    rows = lax.all_to_all(context, "expert", 0, 0, tiled=True)
    rows = rows.reshape(experts * local_requests, latent)
    heads = jnp.dot(rows, value_up_weight[0], preferred_element_type=F32).astype(BF)

    n_rows = heads.shape[0]
    r = jnp.arange(n_rows)
    dc, dy, dx, k = r // 32, (r // 8) % 4, (r // 2) % 4, r % 2
    source = (((y + dy) % 4) * 8 + ((x + dx) % 4) * 2 + (c ^ dc)) * 2 + k
    pick = (source[:, None] == jnp.arange(n_rows)[None, :]).astype(BF)
    heads = jnp.dot(pick, heads, preferred_element_type=F32).astype(BF)
    half = n_rows // 2
    away = jnp.dot(heads[half:], out_proj, preferred_element_type=F32).astype(BF)
    away = plane(away, core=1)
    acc = jnp.dot(heads[:half], out_proj, preferred_element_type=F32) + away.astype(F32)
    attended = tensor_sum(scatter_sum(acc)) + residual_in.astype(F32)

    mean_square = jnp.mean(attended * attended, axis=1, keepdims=True)
    normed = (attended * lax.rsqrt(mean_square + 1e-06) * norm_gain.astype(F32)).astype(BF)
    names = jnp.arange(128, dtype=jnp.int32)
    table = jnp.sum(
        jnp.where(
            expert_ids[:, :, None] == names[None, None, :],
            route_weights.astype(F32)[:, :, None],
            0.0,
        ),
        axis=1,
    ).astype(BF)
    block = jnp.concatenate([normed, table], axis=1)
    block = jnp.concatenate([block, other_role(block)], axis=0)
    for axis in ("right", "down"):
        got = {s: plane(block, **{axis: -s}) for s in (2, 1, 3)}
        block = jnp.concatenate([block, got[1], got[2], got[3]], axis=0)
    across = plane(block, core=1)

    width = normed.shape[1]

    def expert_rows(block):
        rows = block[:, :width]
        coef = jnp.sum(
            jnp.where(names[None, :] == e, block[:, width:].astype(F32), 0.0), axis=1
        )
        gate = jnp.dot(rows, gate_proj[0], preferred_element_type=F32)
        upper = jnp.dot(rows, up_proj[0], preferred_element_type=F32)
        act = (jax.nn.silu(gate) * upper).astype(BF)
        return coef[:, None] * jnp.dot(act, down_proj[0], preferred_element_type=F32)

    sent = plane(expert_rows(across).astype(BF), core=1)
    acc = scatter_sum(expert_rows(block) + sent.astype(F32))
    keep = acc.shape[0] // 2
    acc = acc[:keep] + other_role(acc[keep:].astype(BF)).astype(F32)
    routed = tensor_sum(acc)
    return (attended, routed)


def solution(mesh):
    placed = (
        P(("role", "expert"), "tensor", None),
        P(("role", "expert"), None, None),
        P(("role", "expert")),
        P(("role", "expert"), None),
        P(("expert", "tensor"), None, None),
        P(("expert", "tensor"), None),
        P(),
        P("expert", None, ("role", "tensor")),
        P("expert", None, ("role", "tensor")),
        P("expert", ("role", "tensor"), None),
        P(("role", "expert"), None),
        P(("role", "expert"), None),
    )
    return jax.shard_map(
        shards,
        mesh=mesh,
        in_specs=placed,
        out_specs=(P(("role", "expert"), None), P(("role", "expert"), None)),
        check_vma=False,
    )
```

```python
import jax
import jax.numpy as jnp
from jax import lax
from jax.experimental import pallas as pl
from jax.experimental.pallas import tpu as pltpu
from jax.sharding import PartitionSpec as P

SCORE_SCALE = 192.0 ** (-0.5)
SIDE = 4
BF = jnp.bfloat16
T_AT, CORE_AT, ROLE_AT, EXPERT_AT = range(4)
F32 = jnp.float32


PLANE = ("y", "x")
LINE = ("role", "tensor")


def other_core(value):
    return lax.ppermute(value, "core", [(0, 1), (1, 0)])


def trade(value, axes):
    return lax.all_to_all(value, axes, 0, 0, tiled=True)


def in_three(value):
    high = value.astype(BF).astype(F32)
    rest = value - high
    middle = rest.astype(BF).astype(F32)
    return high, middle, rest - middle


def attend(where_ref, length_ref, q_ref, keys_ref, out_ref):
    heads, slots = q_ref.shape[2], keys_ref.shape[2]
    latent = out_ref.shape[3] - 128
    experts = out_ref.shape[2]
    row = lax.broadcasted_iota(jnp.int32, (heads, heads), 0)
    column = lax.broadcasted_iota(jnp.int32, (heads, heads), 1)
    pick = (column == (row % experts) * 4 + row // experts).astype(BF)
    q = lax.dot_general(pick, q_ref[0], (((1,), (1,)), ((), ())), preferred_element_type=F32)
    logits = jnp.dot(q.astype(BF), keys_ref[0], preferred_element_type=F32) * SCORE_SCALE
    position = where_ref[T_AT] * slots + lax.broadcasted_iota(jnp.int32, (1, slots), 1)
    live = position < length_ref[pl.program_id(0)]
    masked = jnp.where(live, logits, -1e30)
    top = jnp.max(masked, axis=1, keepdims=True)
    expo = jnp.where(live, jnp.exp(masked - top), 0.0)
    total = jnp.sum(expo, axis=1, keepdims=True)
    numer = lax.dot_general(
        expo.astype(BF), keys_ref[0, :latent], (((1,), (1,)), ((), ())), preferred_element_type=F32
    )
    part = (numer / jnp.maximum(total, 1.0)).astype(BF)
    out_ref[:, 0, :, :latent] = part.reshape(4, experts, latent)
    lane = lax.broadcasted_iota(jnp.int32, (heads, 128), 1)
    stats = jnp.zeros((heads, 128), F32)
    for i, column in enumerate((*in_three(top), *in_three(total))):
        stats = jnp.where(lane == i, column, stats)
    out_ref[:, 0, :, latent:] = stats.astype(BF).reshape(4, experts, 128)


def combine(parts_ref, out_ref):
    latent = out_ref.shape[2]
    for r in range(out_ref.shape[0]):
        tops, totals = [], []
        for t in range(4):
            s = parts_ref[t, r, :, latent:].astype(F32)
            tops.append(s[:, 0:1] + s[:, 1:2] + s[:, 2:3])
            totals.append(s[:, 3:4] + s[:, 4:5] + s[:, 5:6])
        top = jnp.maximum(jnp.maximum(tops[0], tops[1]), jnp.maximum(tops[2], tops[3]))
        weights = [jnp.exp(a - top) * b for a, b in zip(tops, totals)]
        whole = weights[0] + weights[1] + weights[2] + weights[3]
        acc = jnp.zeros((out_ref.shape[1], latent), F32)
        for t in range(4):
            acc = acc + (weights[t] / whole) * parts_ref[t, r, :, :latent].astype(F32)
        out_ref[r] = acc.astype(BF)


def pick_part(parts, count, part):
    value = parts[0]
    for j in range(1, count):
        value = jnp.where(part == j, parts[j], value)
    return value


def project(where_ref, rows_ref, value_ref, out_proj_ref, away_ref, own_ref):
    n = rows_ref.shape[0]
    heads = jnp.dot(rows_ref[...], value_ref[0], preferred_element_type=F32).astype(BF)
    out_rows, width = own_ref.shape
    r = lax.broadcasted_iota(jnp.int32, (out_rows, n), 0)
    source = lax.broadcasted_iota(jnp.int32, (out_rows, n), 1)
    quarter = lax.broadcasted_iota(jnp.int32, (out_rows, 1), 0) // 2 % 4
    for dc, out_ref in ((1, away_ref), (0, own_ref)):
        core = (where_ref[CORE_AT] + dc) % 2
        pick = (source == (r // 8) * 4 + core * 2 + r % 2).astype(BF)
        picked = jnp.dot(pick, heads, preferred_element_type=F32).astype(BF)
        for k in range(0, width, 256):
            parts = [
                jnp.dot(
                    picked,
                    out_proj_ref[:, j * width + k : j * width + k + 256],
                    preferred_element_type=F32,
                )
                for j in range(4)
            ]
            out_ref[:, k : k + 256] = pick_part(parts, 4, quarter).astype(out_ref.dtype)


def gather_sum(where_ref, got_ref, extra_ref, table_ref, out_ref, held_ref):
    width = held_ref.shape[1]
    acc = got_ref[0].astype(F32)
    for p in range(1, got_ref.shape[0]):
        acc = acc + got_ref[p].astype(F32)
    held_ref[...] = acc
    first = (where_ref[T_AT] == 0).astype(F32)
    for j in range(4):
        columns = slice(j * width, (j + 1) * width)
        piece = (held_ref[2 * j : 2 * j + 2] + first * extra_ref[:, columns].astype(F32)).astype(BF)
        for z in range(out_ref.shape[0]):
            out_ref[z, :, columns] = piece
    for z in range(out_ref.shape[0]):
        out_ref[z, :, 4 * width :] = table_ref[...]


def normalise(where_ref, got_ref, gain_ref, attended_ref, out_ref, held_ref):
    width = attended_ref.shape[1]
    half = width // 2
    gain = gain_ref[...].astype(F32)
    both = []
    for role in range(2):
        acc = got_ref[4 * role, :, :width].astype(F32)
        for t in range(1, 4):
            acc = acc + got_ref[4 * role + t, :, :width].astype(F32)
        both.append(acc)
        mean_square = jnp.mean(acc * acc, axis=1, keepdims=True)
        normed = acc * lax.rsqrt(mean_square + 1e-06) * gain
        table = got_ref[4 * role, :, width:].astype(F32)
        for h in range(2):
            at = 4 * h + 2 * role
            held_ref[at : at + 2, :half] = normed[:, h * half : (h + 1) * half]
            held_ref[at : at + 2, half:] = table
    attended_ref[...] = jnp.where(where_ref[ROLE_AT] == 0, both[0], both[1])
    block = held_ref[...].astype(BF)
    for p in range(out_ref.shape[0]):
        out_ref[p] = block


def spread_sum(got_ref, out_ref, held_ref):
    half = held_ref.shape[1]
    acc = got_ref[0].astype(F32)
    for p in range(1, got_ref.shape[0]):
        acc = acc + got_ref[p].astype(F32)
    held_ref[...] = acc
    for role in range(2):
        for h in range(2):
            at = 4 * h + 2 * role
            piece = held_ref[at : at + 2].astype(BF)
            for t in range(4):
                out_ref[4 * role + t, :, h * half : (h + 1) * half] = piece


def which_half(rows):
    return lax.broadcasted_iota(jnp.int32, (rows, 1), 0) // 4 % 2


def hidden(where_ref, rows_ref, gate_ref, up_ref):
    n, step = rows_ref.shape[0], 512
    width = gate_ref.shape[1] // 2
    half = which_half(n)

    def whole(ref):
        sums = [jnp.zeros((n, ref.shape[2]), F32) for _ in range(2)]
        for k in range(0, width, step):
            rows = rows_ref[:, k : k + step]
            for h in range(2):
                weights = ref[0, h * width + k : h * width + k + step]
                sums[h] = sums[h] + jnp.dot(rows, weights, preferred_element_type=F32)
        value = pick_part(sums, 2, half)
        other = jnp.where(half == 0, pltpu.roll(value, n - 4, 0), pltpu.roll(value, 4, 0))
        return value + other

    gate, upper = whole(gate_ref), whole(up_ref)
    lane = lax.broadcasted_iota(jnp.int32, (n, 128), 1)
    chosen = jnp.where(lane == where_ref[EXPERT_AT], rows_ref[:, width:].astype(F32), 0.0)
    coef = jnp.sum(chosen, axis=1, keepdims=True)
    act = (gate / (1.0 + jnp.exp(-gate)) * upper).astype(BF)
    return act, coef


def fall(act, coef, down_ref, out_ref):
    width, step = out_ref.shape[1], 512
    half = which_half(act.shape[0])
    for at in range(0, width, step):
        parts = [
            jnp.dot(act, down_ref[0, :, k : k + step], preferred_element_type=F32)
            for k in (at, width + at)
        ]
        out_ref[:, at : at + step] = (coef * pick_part(parts, 2, half)).astype(out_ref.dtype)


def activate(where_ref, rows_ref, gate_ref, up_ref, act_ref, coef_ref):
    act, coef = hidden(where_ref, rows_ref, gate_ref, up_ref)
    act_ref[...] = act
    coef_ref[...] = jnp.broadcast_to(coef, coef_ref.shape)


def through(where_ref, rows_ref, gate_ref, up_ref, down_ref, out_ref):
    act, coef = hidden(where_ref, rows_ref, gate_ref, up_ref)
    fall(act, coef, down_ref, out_ref)


def descend(act_ref, coef_ref, down_ref, out_ref):
    fall(act_ref[...], coef_ref[:, :1], down_ref, out_ref)


SCALAR = pl.BlockSpec(memory_space=pltpu.SMEM)
WHOLE = pl.BlockSpec(memory_space=pltpu.VMEM)


def kernel(body, shapes, inputs, specs=None, scratch=(), work=(0, 0), mib=12):
    return pl.pallas_call(
        body,
        out_shape=shapes,
        in_specs=specs or [WHOLE] * len(inputs),
        out_specs=jax.tree.map(lambda _: WHOLE, shapes),
        scratch_shapes=list(scratch),
        compiler_params=pltpu.CompilerParams(vmem_limit_bytes=mib * 1024 * 1024),
        cost_estimate=pl.CostEstimate(flops=work[0], bytes_accessed=work[1], transcendentals=0),
    )(*inputs)


def shards(
    request_latent_cache,
    queries,
    cache_lengths,
    residual_in,
    value_up_weight,
    out_proj,
    norm_gain,
    gate_proj,
    up_proj,
    down_proj,
    expert_ids,
    route_weights,
):
    t = lax.axis_index("tensor")
    role = lax.axis_index("role")
    c = lax.axis_index("core")
    e = lax.axis_index(("y", "x", "core"))
    where = jnp.stack([t, c, role, e])
    local_requests = request_latent_cache.shape[0]
    latent = value_up_weight.shape[1]
    experts, width = 32, residual_in.shape[1]

    slots, depth = request_latent_cache.shape[1:]
    n_heads = queries.shape[1]
    parts = pl.pallas_call(
        attend,
        grid=(local_requests,),
        out_shape=jax.ShapeDtypeStruct((4, local_requests, experts, latent + 128), BF),
        in_specs=[
            SCALAR,
            SCALAR,
            pl.BlockSpec((1, depth, n_heads), lambda r: (r, 0, 0)),
            pl.BlockSpec((1, depth, slots), lambda r: (r, 0, 0)),
        ],
        out_specs=pl.BlockSpec((4, 1, experts, latent + 128), lambda r: (0, r, 0, 0)),
        compiler_params=pltpu.CompilerParams(vmem_limit_bytes=58 * 1024 * 1024),
    )(
        where,
        cache_lengths,
        jnp.swapaxes(queries, 1, 2),
        jnp.swapaxes(request_latent_cache, 1, 2),
    )
    parts = trade(parts, "tensor")
    context = kernel(
        combine, jax.ShapeDtypeStruct((local_requests, experts, latent), BF), [parts]
    )
    rows = trade(jnp.swapaxes(context, 0, 1), ("y", "x", "core"))
    rows = rows.reshape(experts * local_requests, latent)
    shape = jax.ShapeDtypeStruct
    places, packed = 16, 4 * local_requests
    quarter, middle = width // 4, width // 2
    away, acc = kernel(
        project,
        (shape((places * packed, quarter), BF), shape((places * packed, quarter), F32)),
        [where, rows, value_up_weight, out_proj],
        specs=[SCALAR, WHOLE, WHOLE, WHOLE],
    )
    acc = (acc + other_core(away).astype(F32)).astype(BF)
    acc = trade(acc.reshape(places, packed, quarter), PLANE)
    names = jnp.arange(128, dtype=jnp.int32)
    table = jnp.sum(
        jnp.where(
            expert_ids[:, :, None] == names[None, None, :],
            route_weights.astype(F32)[:, :, None],
            0.0,
        ),
        axis=1,
    ).astype(BF)
    block = kernel(
        gather_sum,
        shape((8, local_requests, width + 128), BF),
        [where, acc, residual_in, table],
        specs=[SCALAR, WHOLE, WHOLE, WHOLE],
        scratch=[pltpu.VMEM((packed, quarter), F32)],
    )
    block = trade(block, LINE)
    attended, block = kernel(
        normalise,
        (
            shape((local_requests, width), F32),
            shape((places, packed, middle + 128), BF),
        ),
        [where, block, norm_gain[None]],
        specs=[SCALAR, WHOLE, WHOLE],
        scratch=[pltpu.VMEM((packed, middle + 128), F32)],
    )
    block = trade(block, PLANE).reshape(places * packed, middle + 128)
    across = other_core(block)

    n_rows, units = block.shape[0], gate_proj.shape[2]
    flops, size = 2 * n_rows * width * units, 2 * width * units
    act, coef = kernel(
        activate,
        (shape((n_rows, units), BF), shape((n_rows, 128), F32)),
        [where, block, gate_proj, up_proj],
        specs=[SCALAR, WHOLE, WHOLE, WHOLE],
        work=(2 * flops, 2 * size),
    )
    across, act, coef = lax.optimization_barrier((across, act, coef))
    sent = kernel(
        through,
        shape((n_rows, middle), BF),
        [where, across, gate_proj, up_proj, down_proj],
        specs=[SCALAR, WHOLE, WHOLE, WHOLE, WHOLE],
        work=(3 * flops, 3 * size),
    )
    sent = other_core(sent)
    acc = kernel(
        descend,
        shape((n_rows, middle), F32),
        [act, coef, down_proj],
        work=(flops, size),
    )
    acc = (acc + sent.astype(F32)).astype(BF)
    acc = trade(acc.reshape(places, packed, middle), PLANE)
    acc = kernel(
        spread_sum,
        shape((8, local_requests, width), BF),
        [acc],
        scratch=[pltpu.VMEM((packed, middle), F32)],
    )
    acc = trade(acc, LINE)
    routed = jnp.sum(acc.astype(F32), axis=0)
    return (attended, routed)


def solution(mesh):
    sizes = (mesh.shape["role"], SIDE, SIDE, 2, mesh.shape["tensor"])
    names = ("role", "y", "x", "core", "tensor")
    expert = ("y", "x", "core")
    own = ("role",) + expert
    placed = (
        P(own, "tensor", None),
        P(own, None, None),
        P(own),
        P(own, None),
        P(expert + ("tensor",), None, None),
        P(expert + ("tensor",), None),
        P(),
        P(expert, None, ("role", "tensor")),
        P(expert, None, ("role", "tensor")),
        P(expert, ("role", "tensor"), None),
        P(own, None),
        P(own, None),
    )
    return jax.shard_map(
        shards,
        mesh=jax.sharding.Mesh(mesh.devices.reshape(sizes), names),
        in_specs=placed,
        out_specs=(P(own, None), P(own, None)),
        check_vma=False,
    )
```

```python
import functools

import jax
import jax.numpy as jnp
from jax import lax
from jax.experimental import pallas as pl
from jax.experimental.pallas import tpu as pltpu
from jax.sharding import PartitionSpec as P

SCORE_SCALE = 192.0 ** (-0.5)
SIDE = 4
BF = jnp.bfloat16
F32 = jnp.float32


PLANE = ("y", "x")
LINE = ("role", "tensor")


def other_core(value):
    return lax.ppermute(value, "core", [(0, 1), (1, 0)])


def along(value, bits):
    return lax.ppermute(value, LINE, [(i, i ^ bits) for i in range(8)])


def trade(value, axes):
    return lax.all_to_all(value, axes, 0, 0, tiled=True)


def in_three(value):
    high = value.astype(BF).astype(F32)
    rest = value - high
    middle = rest.astype(BF).astype(F32)
    return high, middle, rest - middle


def attend(length_ref, q_ref, keys_ref, out_ref):
    heads, slots = q_ref.shape[2], keys_ref.shape[2]
    latent = out_ref.shape[3] - 128
    experts = out_ref.shape[2]
    row = lax.broadcasted_iota(jnp.int32, (heads, heads), 0)
    column = lax.broadcasted_iota(jnp.int32, (heads, heads), 1)
    pick = (column == (row % experts) * 4 + row // experts).astype(BF)
    q = lax.dot_general(pick, q_ref[0], (((1,), (1,)), ((), ())), preferred_element_type=F32)
    logits = jnp.dot(q.astype(BF), keys_ref[0], preferred_element_type=F32) * SCORE_SCALE
    position = lax.axis_index("tensor") * slots + lax.broadcasted_iota(jnp.int32, (1, slots), 1)
    live = position < length_ref[pl.program_id(0)]
    masked = jnp.where(live, logits, -1e30)
    top = jnp.max(masked, axis=1, keepdims=True)
    expo = jnp.where(live, jnp.exp(masked - top), 0.0)
    total = jnp.sum(expo, axis=1, keepdims=True)
    numer = lax.dot_general(
        expo.astype(BF), keys_ref[0, :latent], (((1,), (1,)), ((), ())), preferred_element_type=F32
    )
    part = (numer / jnp.maximum(total, 1.0)).astype(BF)
    out_ref[:, 0, :, :latent] = part.reshape(4, experts, latent)
    lane = lax.broadcasted_iota(jnp.int32, (heads, 128), 1)
    stats = jnp.zeros((heads, 128), F32)
    for i, column in enumerate((*in_three(top), *in_three(total))):
        stats = jnp.where(lane == i, column, stats)
    out_ref[:, 0, :, latent:] = stats.astype(BF).reshape(4, experts, 128)


def combine(parts_ref, out_ref):
    latent = out_ref.shape[2]
    for r in range(out_ref.shape[0]):
        tops, totals = [], []
        for t in range(4):
            s = parts_ref[t, r, :, latent:].astype(F32)
            tops.append(s[:, 0:1] + s[:, 1:2] + s[:, 2:3])
            totals.append(s[:, 3:4] + s[:, 4:5] + s[:, 5:6])
        top = jnp.maximum(jnp.maximum(tops[0], tops[1]), jnp.maximum(tops[2], tops[3]))
        weights = [jnp.exp(a - top) * b for a, b in zip(tops, totals)]
        whole = weights[0] + weights[1] + weights[2] + weights[3]
        acc = jnp.zeros((out_ref.shape[1], latent), F32)
        for t in range(4):
            acc = acc + (weights[t] / whole) * parts_ref[t, r, :, :latent].astype(F32)
        out_ref[r] = acc.astype(BF)


def pick_part(parts, count, part):
    value = parts[0]
    for j in range(1, count):
        value = jnp.where(part == j, parts[j], value)
    return value


def project(dc, rows_ref, value_ref, out_proj_ref, out_ref):
    n = rows_ref.shape[0]
    heads = jnp.dot(rows_ref[...], value_ref[0], preferred_element_type=F32).astype(BF)
    out_rows, width = out_ref.shape
    r = lax.broadcasted_iota(jnp.int32, (out_rows, n), 0)
    source = lax.broadcasted_iota(jnp.int32, (out_rows, n), 1)
    quarter = lax.broadcasted_iota(jnp.int32, (out_rows, 1), 0) // 2 % 4
    core = (lax.axis_index("core") + dc) % 2
    pick = (source == (r // 8) * 4 + core * 2 + r % 2).astype(BF)
    picked = jnp.dot(pick, heads, preferred_element_type=F32).astype(BF)
    for k in range(0, width, 256):
        parts = [
            jnp.dot(
                picked,
                out_proj_ref[:, j * width + k : j * width + k + 256],
                preferred_element_type=F32,
            )
            for j in range(4)
        ]
        out_ref[:, k : k + 256] = pick_part(parts, 4, quarter).astype(out_ref.dtype)


def add_places(got_ref):
    acc = got_ref[0].astype(F32)
    for p in range(1, got_ref.shape[0]):
        acc = acc + got_ref[p].astype(F32)
    return acc


def gather_sum(got_ref, extra_ref, ids_ref, weights_ref, out_ref, held_ref):
    width = held_ref.shape[1]
    held_ref[...] = add_places(got_ref)
    first = (lax.axis_index("tensor") == 0).astype(F32)
    for j in range(4):
        columns = slice(j * width, (j + 1) * width)
        term = first * extra_ref[:, columns].astype(F32)
        out_ref[:, columns] = (held_ref[2 * j : 2 * j + 2] + term).astype(BF)
    ids, weights = ids_ref[...], weights_ref[...].astype(F32)
    lane = lax.broadcasted_iota(jnp.int32, (ids.shape[0], 128), 1)
    table = jnp.zeros(lane.shape, F32)
    for k in range(ids.shape[1]):
        table = table + jnp.where(lane == ids[:, k : k + 1], weights[:, k : k + 1], 0.0)
    out_ref[:, 4 * width :] = table.astype(BF)


def add_pair(here_ref, there_ref, out_ref):
    width = here_ref.shape[1] - 128
    both = here_ref[:, :width].astype(F32) + there_ref[:, :width].astype(F32)
    out_ref[:, :width] = both.astype(BF)
    out_ref[:, width:] = here_ref[:, width:]


def normalise(a_ref, b_ref, c_ref, d_ref, gain_ref, attended_ref, out_ref, held_ref):
    width = attended_ref.shape[1]
    half = width // 2
    gain = gain_ref[...].astype(F32).reshape(1, width)
    for role, (here_ref, there_ref) in enumerate(((a_ref, b_ref), (c_ref, d_ref))):
        acc = here_ref[:, :width].astype(F32) + there_ref[:, :width].astype(F32)
        if role == 0:
            attended_ref[...] = acc
        mean_square = jnp.mean(acc * acc, axis=1, keepdims=True)
        normed = acc * lax.rsqrt(mean_square + 1e-06) * gain
        table = here_ref[:, width:].astype(F32)
        for h in range(2):
            at = 4 * h + 2 * role
            held_ref[at : at + 2, :half] = normed[:, h * half : (h + 1) * half]
            held_ref[at : at + 2, half:] = table
    block = held_ref[...].astype(BF)
    for p in range(out_ref.shape[0]):
        out_ref[p] = block


def spread_sum(got_ref, out_ref, held_ref):
    half = held_ref.shape[1]
    held_ref[...] = add_places(got_ref)
    first = lax.axis_index("role") == 0
    for h in range(2):
        columns = slice(h * half, (h + 1) * half)
        own = held_ref[4 * h : 4 * h + 2]
        other = held_ref[4 * h + 2 : 4 * h + 4]
        low = jnp.where(first, own, other).astype(BF)
        high = jnp.where(first, other, own).astype(BF)
        for t in range(4):
            out_ref[t, :, columns] = low
            out_ref[4 + t, :, columns] = high


def which_half(rows):
    return lax.broadcasted_iota(jnp.int32, (rows, 1), 0) // 4 % 2


def hidden(rows_ref, gate_ref, up_ref):
    n, step = rows_ref.shape[0], 512
    width = gate_ref.shape[1] // 2
    half = which_half(n)

    def whole(ref):
        sums = [jnp.zeros((n, ref.shape[2]), F32) for _ in range(2)]
        for k in range(0, width, step):
            rows = rows_ref[:, k : k + step]
            for h in range(2):
                weights = ref[0, h * width + k : h * width + k + step]
                sums[h] = sums[h] + jnp.dot(rows, weights, preferred_element_type=F32)
        value = pick_part(sums, 2, half)
        other = jnp.where(half == 0, pltpu.roll(value, n - 4, 0), pltpu.roll(value, 4, 0))
        return value + other

    gate, upper = whole(gate_ref), whole(up_ref)
    lane = lax.broadcasted_iota(jnp.int32, (n, 128), 1)
    chosen = jnp.where(lane == lax.axis_index(("y", "x", "core")), rows_ref[:, width:].astype(F32), 0.0)
    coef = jnp.sum(chosen, axis=1, keepdims=True)
    act = (gate / (1.0 + jnp.exp(-gate)) * upper).astype(BF)
    return act, coef


def fall(act, coef, down_ref, out_ref):
    width, step = out_ref.shape[1], 512
    half = which_half(act.shape[0])
    for at in range(0, width, step):
        parts = [
            jnp.dot(act, down_ref[0, :, k : k + step], preferred_element_type=F32)
            for k in (at, width + at)
        ]
        out_ref[:, at : at + step] = (coef * pick_part(parts, 2, half)).astype(out_ref.dtype)


def activate(rows_ref, gate_ref, up_ref, act_ref, coef_ref):
    act, coef = hidden(rows_ref, gate_ref, up_ref)
    act_ref[...] = act
    coef_ref[...] = jnp.broadcast_to(coef, coef_ref.shape)


def through(rows_ref, gate_ref, up_ref, down_ref, out_ref):
    act, coef = hidden(rows_ref, gate_ref, up_ref)
    fall(act, coef, down_ref, out_ref)


def descend(act_ref, coef_ref, down_ref, out_ref):
    fall(act_ref[...], coef_ref[:, :1], down_ref, out_ref)


SCALAR = pl.BlockSpec(memory_space=pltpu.SMEM)
WHOLE = pl.BlockSpec(memory_space=pltpu.VMEM)


def kernel(body, shapes, inputs, specs=None, scratch=(), work=(0, 0), mib=12):
    return pl.pallas_call(
        body,
        out_shape=shapes,
        in_specs=specs or [WHOLE] * len(inputs),
        out_specs=jax.tree.map(lambda _: WHOLE, shapes),
        scratch_shapes=list(scratch),
        compiler_params=pltpu.CompilerParams(vmem_limit_bytes=mib * 1024 * 1024),
        cost_estimate=pl.CostEstimate(flops=work[0], bytes_accessed=work[1], transcendentals=0),
    )(*inputs)


def shards(
    request_latent_cache,
    queries,
    cache_lengths,
    residual_in,
    value_up_weight,
    out_proj,
    norm_gain,
    gate_proj,
    up_proj,
    down_proj,
    expert_ids,
    route_weights,
):
    local_requests = request_latent_cache.shape[0]
    latent = value_up_weight.shape[1]
    experts, width = 32, residual_in.shape[1]

    slots, depth = request_latent_cache.shape[1:]
    n_heads = queries.shape[1]
    parts = pl.pallas_call(
        attend,
        grid=(local_requests,),
        out_shape=jax.ShapeDtypeStruct((4, local_requests, experts, latent + 128), BF),
        in_specs=[
            SCALAR,
            pl.BlockSpec((1, depth, n_heads), lambda r: (r, 0, 0)),
            pl.BlockSpec((1, depth, slots), lambda r: (r, 0, 0)),
        ],
        out_specs=pl.BlockSpec((4, 1, experts, latent + 128), lambda r: (0, r, 0, 0)),
        compiler_params=pltpu.CompilerParams(vmem_limit_bytes=58 * 1024 * 1024),
    )(
        cache_lengths,
        jnp.swapaxes(queries, 1, 2),
        jnp.swapaxes(request_latent_cache, 1, 2),
    )
    parts = trade(parts, "tensor")
    context = kernel(
        combine, jax.ShapeDtypeStruct((local_requests, experts, latent), BF), [parts]
    )
    rows = trade(jnp.swapaxes(context, 0, 1), ("y", "x", "core"))
    rows = rows.reshape(experts * local_requests, latent)
    shape = jax.ShapeDtypeStruct
    places, packed = 16, 4 * local_requests
    quarter, middle = width // 4, width // 2
    away, acc = [
        kernel(
            functools.partial(project, dc),
            shape((places * packed, quarter), kind),
            [rows, value_up_weight, out_proj],
            work=(2 * places * packed * 128 * width, 2 * 128 * width),
        )
        for dc, kind in ((1, BF), (0, F32))
    ]
    acc = (acc + other_core(away).astype(F32)).astype(BF)
    acc = trade(acc.reshape(places, packed, quarter), PLANE)
    routed_width = width + 128
    block = kernel(
        gather_sum,
        shape((local_requests, routed_width), BF),
        [acc, residual_in, expert_ids, route_weights],
        scratch=[pltpu.VMEM((packed, quarter), F32)],
    )
    block = kernel(
        add_pair, shape((local_requests, routed_width), BF), [block, along(block, 1)]
    )
    far, near, mate = along(block, 5), along(block, 6), along(block, 2)
    attended, block = kernel(
        normalise,
        (
            shape((local_requests, width), F32),
            shape((places, packed, middle + 128), BF),
        ),
        [block, mate, near, far, norm_gain],
        scratch=[pltpu.VMEM((packed, middle + 128), F32)],
    )
    block = trade(block, PLANE).reshape(places * packed, middle + 128)
    across = other_core(block)

    n_rows, units = block.shape[0], gate_proj.shape[2]
    flops, size = 2 * n_rows * width * units, 2 * width * units
    act, coef = kernel(
        activate,
        (shape((n_rows, units), BF), shape((n_rows, 128), F32)),
        [block, gate_proj, up_proj],
        work=(2 * flops, 2 * size),
    )
    across, act, coef = lax.optimization_barrier((across, act, coef))
    sent = kernel(
        through,
        shape((n_rows, middle), BF),
        [across, gate_proj, up_proj, down_proj],
        work=(3 * flops, 3 * size),
    )
    sent = other_core(sent)
    acc = kernel(
        descend,
        shape((n_rows, middle), F32),
        [act, coef, down_proj],
        work=(flops, size),
    )
    acc = (acc + sent.astype(F32)).astype(BF)
    acc = trade(acc.reshape(places, packed, middle), PLANE)
    acc = kernel(
        spread_sum,
        shape((8, local_requests, width), BF),
        [acc],
        scratch=[pltpu.VMEM((packed, middle), F32)],
    )
    acc = trade(acc, LINE)
    routed = jnp.sum(acc.astype(F32), axis=0)
    return (attended, routed)


def solution(mesh):
    sizes = (mesh.shape["role"], SIDE, SIDE, 2, mesh.shape["tensor"])
    names = ("role", "y", "x", "core", "tensor")
    expert = ("y", "x", "core")
    own = ("role",) + expert
    placed = (
        P(own, "tensor", None),
        P(own, None, None),
        P(own),
        P(own, None),
        P(expert + ("tensor",), None, None),
        P(expert + ("tensor",), None),
        P(),
        P(expert, None, ("role", "tensor")),
        P(expert, None, ("role", "tensor")),
        P(expert, ("role", "tensor"), None),
        P(own, None),
        P(own, None),
    )
    return jax.shard_map(
        shards,
        mesh=jax.sharding.Mesh(mesh.devices.reshape(sizes), names),
        in_specs=placed,
        out_specs=(P(own, None), P(own, None)),
        check_vma=False,
    )
```

```python
import functools

import jax
import jax.numpy as jnp
from jax import lax
from jax.experimental import pallas as pl
from jax.experimental.pallas import tpu as pltpu
from jax.sharding import PartitionSpec as P

SCORE_SCALE = 192.0 ** (-0.5)
SIDE = 4
BF = jnp.bfloat16
F32 = jnp.float32


PLANE = ("y", "x")
LINE = ("role", "tensor")


def other_core(value):
    return lax.ppermute(value, "core", [(0, 1), (1, 0)])


def along(value, bits):
    return lax.ppermute(value, LINE, [(i, i ^ bits) for i in range(8)])


def trade(value, axes):
    return lax.all_to_all(value, axes, 0, 0, tiled=True)


def in_three(value):
    high = value.astype(BF).astype(F32)
    rest = value - high
    middle = rest.astype(BF).astype(F32)
    return high, middle, rest - middle


def attend(length_ref, q_ref, keys_ref, *out_refs):
    heads, slots = q_ref.shape[2], keys_ref.shape[2]
    latent = out_refs[0].shape[2] - 128
    experts = out_refs[0].shape[1]
    row = lax.broadcasted_iota(jnp.int32, (heads, heads), 0)
    column = lax.broadcasted_iota(jnp.int32, (heads, heads), 1)
    owner = (lax.axis_index("tensor") + row // experts) % 4
    pick = (column == (row % experts) * 4 + owner).astype(BF)
    q = lax.dot_general(pick, q_ref[0], (((1,), (1,)), ((), ())), preferred_element_type=F32)
    logits = jnp.dot(q.astype(BF), keys_ref[0], preferred_element_type=F32) * SCORE_SCALE
    position = lax.axis_index("tensor") * slots + lax.broadcasted_iota(jnp.int32, (1, slots), 1)
    live = position < length_ref[pl.program_id(0)]
    masked = jnp.where(live, logits, -1e30)
    top = jnp.max(masked, axis=1, keepdims=True)
    expo = jnp.where(live, jnp.exp(masked - top), 0.0)
    total = jnp.sum(expo, axis=1, keepdims=True)
    numer = lax.dot_general(
        expo.astype(BF), keys_ref[0, :latent], (((1,), (1,)), ((), ())), preferred_element_type=F32
    )
    part = (numer / jnp.maximum(total, 1.0)).astype(BF)
    for t, out_ref in enumerate(out_refs):
        out_ref[0, :, :latent] = part[t * experts : (t + 1) * experts]
    lane = lax.broadcasted_iota(jnp.int32, (heads, 128), 1)
    stats = jnp.zeros((heads, 128), F32)
    for i, column in enumerate((*in_three(top), *in_three(total))):
        stats = jnp.where(lane == i, column, stats)
    stats = stats.astype(BF)
    for t, out_ref in enumerate(out_refs):
        out_ref[0, :, latent:] = stats[t * experts : (t + 1) * experts]


def combine(*refs):
    parts_refs, out_ref = refs[:-1], refs[-1]
    experts, requests, latent = out_ref.shape
    contexts = []
    for r in range(requests):
        tops, totals = [], []
        for t in range(4):
            s = parts_refs[t][r, :, latent:].astype(F32)
            tops.append(s[:, 0:1] + s[:, 1:2] + s[:, 2:3])
            totals.append(s[:, 3:4] + s[:, 4:5] + s[:, 5:6])
        top = jnp.maximum(jnp.maximum(tops[0], tops[1]), jnp.maximum(tops[2], tops[3]))
        weights = [jnp.exp(a - top) * b for a, b in zip(tops, totals)]
        whole = weights[0] + weights[1] + weights[2] + weights[3]
        acc = jnp.zeros((experts, latent), F32)
        for t in range(4):
            acc = acc + (weights[t] / whole) * parts_refs[t][r, :, :latent].astype(F32)
        contexts.append(acc)
    out_ref[...] = jnp.stack(contexts, axis=1).astype(BF)


def pick_part(parts, count, part):
    value = parts[0]
    for j in range(1, count):
        value = jnp.where(part == j, parts[j], value)
    return value


def project(dc, rows_ref, value_ref, out_proj_ref, out_ref):
    n = rows_ref.shape[0]
    heads = jnp.dot(rows_ref[...], value_ref[0], preferred_element_type=F32).astype(BF)
    out_rows, width = out_ref.shape
    r = lax.broadcasted_iota(jnp.int32, (out_rows, n), 0)
    source = lax.broadcasted_iota(jnp.int32, (out_rows, n), 1)
    quarter = lax.broadcasted_iota(jnp.int32, (out_rows, 1), 0) // 2 % 4
    core = (lax.axis_index("core") + dc) % 2
    pick = (source == (r // 8) * 4 + core * 2 + r % 2).astype(BF)
    picked = jnp.dot(pick, heads, preferred_element_type=F32).astype(BF)
    for k in range(0, width, 256):
        parts = [
            jnp.dot(
                picked,
                out_proj_ref[:, j * width + k : j * width + k + 256],
                preferred_element_type=F32,
            )
            for j in range(4)
        ]
        out_ref[:, k : k + 256] = pick_part(parts, 4, quarter).astype(out_ref.dtype)


def add_places(got_ref):
    acc = got_ref[0].astype(F32)
    for p in range(1, got_ref.shape[0]):
        acc = acc + got_ref[p].astype(F32)
    return acc


def gather_sum(got_ref, extra_ref, ids_ref, weights_ref, out_ref, held_ref):
    width = held_ref.shape[1]
    held_ref[...] = add_places(got_ref)
    first = (lax.axis_index("tensor") == 0).astype(F32)
    for j in range(4):
        columns = slice(j * width, (j + 1) * width)
        term = first * extra_ref[:, columns].astype(F32)
        out_ref[:, columns] = (held_ref[2 * j : 2 * j + 2] + term).astype(BF)
    ids, weights = ids_ref[...], weights_ref[...].astype(F32)
    lane = lax.broadcasted_iota(jnp.int32, (ids.shape[0], 128), 1)
    table = jnp.zeros(lane.shape, F32)
    for k in range(ids.shape[1]):
        table = table + jnp.where(lane == ids[:, k : k + 1], weights[:, k : k + 1], 0.0)
    out_ref[:, 4 * width :] = table.astype(BF)


def add_pair(here_ref, there_ref, out_ref):
    width = here_ref.shape[1] - 128
    both = here_ref[:, :width].astype(F32) + there_ref[:, :width].astype(F32)
    out_ref[:, :width] = both.astype(BF)
    out_ref[:, width:] = here_ref[:, width:]


def normalise(a_ref, b_ref, c_ref, d_ref, gain_ref, attended_ref, out_ref, held_ref):
    width = attended_ref.shape[1]
    half = width // 2
    gain = gain_ref[...].astype(F32).reshape(1, width)
    for role, (here_ref, there_ref) in enumerate(((a_ref, b_ref), (c_ref, d_ref))):
        acc = here_ref[:, :width].astype(F32) + there_ref[:, :width].astype(F32)
        if role == 0:
            attended_ref[...] = acc
        mean_square = jnp.mean(acc * acc, axis=1, keepdims=True)
        normed = acc * lax.rsqrt(mean_square + 1e-06) * gain
        table = here_ref[:, width:].astype(F32)
        for h in range(2):
            at = 4 * h + 2 * role
            held_ref[at : at + 2, :half] = normed[:, h * half : (h + 1) * half]
            held_ref[at : at + 2, half:] = table
    block = held_ref[...].astype(BF)
    for p in range(out_ref.shape[0]):
        out_ref[p] = block


def spread_sum(got_ref, out_ref, held_ref):
    half = held_ref.shape[1]
    held_ref[...] = add_places(got_ref)
    first = lax.axis_index("role") == 0
    for h in range(2):
        columns = slice(h * half, (h + 1) * half)
        own = held_ref[4 * h : 4 * h + 2]
        other = held_ref[4 * h + 2 : 4 * h + 4]
        low = jnp.where(first, own, other).astype(BF)
        high = jnp.where(first, other, own).astype(BF)
        for t in range(4):
            out_ref[t, :, columns] = low
            out_ref[4 + t, :, columns] = high


def which_half(rows):
    return lax.broadcasted_iota(jnp.int32, (rows, 1), 0) // 4 % 2


def hidden(rows_ref, gate_ref, up_ref):
    n, step = rows_ref.shape[0], 512
    width = gate_ref.shape[1] // 2
    half = which_half(n)

    units = gate_ref.shape[2]
    sums = [jnp.zeros((n, 2 * units), F32) for _ in range(2)]
    for k in range(0, width, step):
        rows = rows_ref[:, k : k + step]
        for h in range(2):
            at = slice(h * width + k, h * width + k + step)
            weights = jnp.concatenate([gate_ref[0, at], up_ref[0, at]], axis=1)
            sums[h] = sums[h] + jnp.dot(rows, weights, preferred_element_type=F32)
    value = pick_part(sums, 2, half)
    other = jnp.where(half == 0, pltpu.roll(value, n - 4, 0), pltpu.roll(value, 4, 0))
    value = value + other
    gate, upper = value[:, :units], value[:, units:]
    lane = lax.broadcasted_iota(jnp.int32, (n, 128), 1)
    chosen = jnp.where(lane == lax.axis_index(("y", "x", "core")), rows_ref[:, width:].astype(F32), 0.0)
    coef = jnp.sum(chosen, axis=1, keepdims=True)
    act = (gate / (1.0 + jnp.exp(-gate)) * upper).astype(BF)
    return act, coef


def fall(act, coef, down_ref, out_ref):
    width, step = out_ref.shape[1], 512
    half = which_half(act.shape[0])
    for at in range(0, width, step):
        parts = [
            jnp.dot(act, down_ref[0, :, k : k + step], preferred_element_type=F32)
            for k in (at, width + at)
        ]
        out_ref[:, at : at + step] = (coef * pick_part(parts, 2, half)).astype(out_ref.dtype)


def activate(rows_ref, gate_ref, up_ref, act_ref, coef_ref):
    act, coef = hidden(rows_ref, gate_ref, up_ref)
    act_ref[...] = act
    coef_ref[...] = jnp.broadcast_to(coef, coef_ref.shape)


def through(rows_ref, gate_ref, up_ref, down_ref, out_ref):
    act, coef = hidden(rows_ref, gate_ref, up_ref)
    fall(act, coef, down_ref, out_ref)


def descend(act_ref, coef_ref, down_ref, out_ref):
    fall(act_ref[...], coef_ref[:, :1], down_ref, out_ref)


SCALAR = pl.BlockSpec(memory_space=pltpu.SMEM)
WHOLE = pl.BlockSpec(memory_space=pltpu.VMEM)


def kernel(body, shapes, inputs, specs=None, scratch=(), work=(0, 0), mib=12):
    return pl.pallas_call(
        body,
        out_shape=shapes,
        in_specs=specs or [WHOLE] * len(inputs),
        out_specs=jax.tree.map(lambda _: WHOLE, shapes),
        scratch_shapes=list(scratch),
        compiler_params=pltpu.CompilerParams(vmem_limit_bytes=mib * 1024 * 1024),
        cost_estimate=pl.CostEstimate(flops=work[0], bytes_accessed=work[1], transcendentals=0),
    )(*inputs)


def shards(
    request_latent_cache,
    queries,
    cache_lengths,
    residual_in,
    value_up_weight,
    out_proj,
    norm_gain,
    gate_proj,
    up_proj,
    down_proj,
    expert_ids,
    route_weights,
):
    local_requests = request_latent_cache.shape[0]
    latent = value_up_weight.shape[1]
    experts, width = 32, residual_in.shape[1]

    slots, depth = request_latent_cache.shape[1:]
    n_heads = queries.shape[1]
    parts = pl.pallas_call(
        attend,
        grid=(local_requests,),
        out_shape=[pltpu.VMEM((local_requests, experts, latent + 128), BF)] * 4,
        in_specs=[
            SCALAR,
            pl.BlockSpec((1, depth, n_heads), lambda r: (r, 0, 0)),
            pl.BlockSpec((1, depth, slots), lambda r: (r, 0, 0)),
        ],
        out_specs=[pl.BlockSpec((1, experts, latent + 128), lambda r: (r, 0, 0))] * 4,
        compiler_params=pltpu.CompilerParams(vmem_limit_bytes=58 * 1024 * 1024),
    )(
        cache_lengths,
        jnp.swapaxes(queries, 1, 2),
        jnp.swapaxes(request_latent_cache, 1, 2),
    )
    parts = [parts[0]] + [
        lax.ppermute(parts[s], "tensor", [(i, (i + s) % 4) for i in range(4)]) for s in (1, 2, 3)
    ]
    context = kernel(
        combine, jax.ShapeDtypeStruct((experts, local_requests, latent), BF), parts
    )
    rows = trade(context, ("y", "x", "core"))
    rows = rows.reshape(experts * local_requests, latent)
    shape = jax.ShapeDtypeStruct
    places, packed = 16, 4 * local_requests
    quarter, middle = width // 4, width // 2
    away, acc = [
        kernel(
            functools.partial(project, dc),
            shape((places * packed, quarter), kind),
            [rows, value_up_weight, out_proj],
            work=(2 * places * packed * 128 * width, 2 * 128 * width),
        )
        for dc, kind in ((1, BF), (0, F32))
    ]
    acc = (acc + other_core(away).astype(F32)).astype(BF)
    acc = trade(acc.reshape(places, packed, quarter), PLANE)
    routed_width = width + 128
    block = kernel(
        gather_sum,
        shape((local_requests, routed_width), BF),
        [acc, residual_in, expert_ids, route_weights],
        scratch=[pltpu.VMEM((packed, quarter), F32)],
    )
    block = kernel(
        add_pair, shape((local_requests, routed_width), BF), [block, along(block, 1)]
    )
    far, near, mate = along(block, 5), along(block, 6), along(block, 2)
    attended, block = kernel(
        normalise,
        (
            shape((local_requests, width), F32),
            shape((places, packed, middle + 128), BF),
        ),
        [block, mate, near, far, norm_gain],
        scratch=[pltpu.VMEM((packed, middle + 128), F32)],
    )
    block = trade(block, PLANE).reshape(places * packed, middle + 128)
    across = other_core(block)

    n_rows, units = block.shape[0], gate_proj.shape[2]
    flops, size = 2 * n_rows * width * units, 2 * width * units
    act, coef = kernel(
        activate,
        (shape((n_rows, units), BF), shape((n_rows, 128), F32)),
        [block, gate_proj, up_proj],
        work=(2 * flops, 2 * size),
    )
    across, act, coef = lax.optimization_barrier((across, act, coef))
    sent = kernel(
        through,
        shape((n_rows, middle), BF),
        [across, gate_proj, up_proj, down_proj],
        work=(3 * flops, 3 * size),
    )
    sent = other_core(sent)
    acc = kernel(
        descend,
        shape((n_rows, middle), F32),
        [act, coef, down_proj],
        work=(flops, size),
    )
    acc = (acc + sent.astype(F32)).astype(BF)
    acc = trade(acc.reshape(places, packed, middle), PLANE)
    acc = kernel(
        spread_sum,
        shape((8, local_requests, width), BF),
        [acc],
        scratch=[pltpu.VMEM((packed, middle), F32)],
    )
    acc = trade(acc, LINE)
    routed = jnp.sum(acc.astype(F32), axis=0)
    return (attended, routed)


def solution(mesh):
    sizes = (mesh.shape["role"], SIDE, SIDE, 2, mesh.shape["tensor"])
    names = ("role", "y", "x", "core", "tensor")
    expert = ("y", "x", "core")
    own = ("role",) + expert
    placed = (
        P(own, "tensor", None),
        P(own, None, None),
        P(own),
        P(own, None),
        P(expert + ("tensor",), None, None),
        P(expert + ("tensor",), None),
        P(),
        P(expert, None, ("role", "tensor")),
        P(expert, None, ("role", "tensor")),
        P(expert, ("role", "tensor"), None),
        P(own, None),
        P(own, None),
    )
    return jax.shard_map(
        shards,
        mesh=jax.sharding.Mesh(mesh.devices.reshape(sizes), names),
        in_specs=placed,
        out_specs=(P(own, None), P(own, None)),
        check_vma=False,
    )
```

```python
import functools

import jax
import jax.numpy as jnp
from jax import lax
from jax.experimental import pallas as pl
from jax.experimental.pallas import tpu as pltpu
from jax.sharding import PartitionSpec as P

SCORE_SCALE = 192.0 ** (-0.5)
SIDE = 4
BF = jnp.bfloat16
F32 = jnp.float32


PLANE = ("x", "y")
LINE = ("role", "tensor")


def other_core(value):
    return lax.ppermute(value, "core", [(0, 1), (1, 0)])


def along(value, bits):
    return lax.ppermute(value, LINE, [(i, i ^ bits) for i in range(8)])


def trade(value, axes):
    return lax.all_to_all(value, axes, 0, 0, tiled=True)


def in_three(value):
    high = value.astype(BF).astype(F32)
    rest = value - high
    middle = rest.astype(BF).astype(F32)
    return high, middle, rest - middle


def attend(length_ref, q_ref, first_ref, last_ref, *out_refs):
    heads, half = q_ref.shape[2], first_ref.shape[2]
    slots = 2 * half
    latent = out_refs[0].shape[2] - 128
    experts = out_refs[0].shape[1]
    row = lax.broadcasted_iota(jnp.int32, (heads, heads), 0)
    column = lax.broadcasted_iota(jnp.int32, (heads, heads), 1)
    owner = (lax.axis_index("tensor") + row // experts) % 4
    place = row % experts
    expert = (place // 2 % SIDE * SIDE + place // (2 * SIDE)) * 2 + place % 2
    pick = (column == expert * 4 + owner).astype(BF)
    q = lax.dot_general(pick, q_ref[0], (((1,), (1,)), ((), ())), preferred_element_type=F32)
    q = q.astype(BF)
    logits = [
        jnp.dot(q, keys_ref[0], preferred_element_type=F32) for keys_ref in (first_ref, last_ref)
    ]
    logits = jnp.concatenate(logits, axis=1) * SCORE_SCALE
    position = lax.axis_index("tensor") * slots + lax.broadcasted_iota(jnp.int32, (1, slots), 1)
    live = position < length_ref[pl.program_id(0)]
    masked = jnp.where(live, logits, -1e30)
    top = jnp.max(masked, axis=1, keepdims=True)
    expo = jnp.where(live, jnp.exp(masked - top), 0.0)
    total = jnp.sum(expo, axis=1, keepdims=True)
    expo = expo.astype(BF)
    numer = jnp.zeros((heads, latent), F32)
    for part, keys_ref in ((expo[:, :half], first_ref), (expo[:, half:], last_ref)):
        numer = numer + lax.dot_general(
            part, keys_ref[0, :latent], (((1,), (1,)), ((), ())), preferred_element_type=F32
        )
    part = (numer / jnp.maximum(total, 1.0)).astype(BF)
    for t, out_ref in enumerate(out_refs):
        out_ref[0, :, :latent] = part[t * experts : (t + 1) * experts]
    lane = lax.broadcasted_iota(jnp.int32, (heads, 128), 1)
    stats = jnp.zeros((heads, 128), F32)
    for i, column in enumerate((*in_three(top), *in_three(total))):
        stats = jnp.where(lane == i, column, stats)
    stats = stats.astype(BF)
    for t, out_ref in enumerate(out_refs):
        out_ref[0, :, latent:] = stats[t * experts : (t + 1) * experts]


def combine(*refs):
    parts_refs, out_ref = refs[:-1], refs[-1]
    experts, requests, latent = out_ref.shape
    contexts = []
    for r in range(requests):
        tops, totals = [], []
        for t in range(4):
            s = parts_refs[t][r, :, latent:].astype(F32)
            tops.append(s[:, 0:1] + s[:, 1:2] + s[:, 2:3])
            totals.append(s[:, 3:4] + s[:, 4:5] + s[:, 5:6])
        top = jnp.maximum(jnp.maximum(tops[0], tops[1]), jnp.maximum(tops[2], tops[3]))
        weights = [jnp.exp(a - top) * b for a, b in zip(tops, totals)]
        whole = weights[0] + weights[1] + weights[2] + weights[3]
        acc = jnp.zeros((experts, latent), F32)
        for t in range(4):
            acc = acc + (weights[t] / whole) * parts_refs[t][r, :, :latent].astype(F32)
        contexts.append(acc)
    out_ref[...] = jnp.stack(contexts, axis=1).astype(BF)


def pick_part(parts, count, part):
    value = parts[0]
    for j in range(1, count):
        value = jnp.where(part == j, parts[j], value)
    return value


def project(dc, rows_ref, value_ref, out_proj_ref, out_ref):
    n = rows_ref.shape[0]
    heads = jnp.dot(rows_ref[...], value_ref[0], preferred_element_type=F32).astype(BF)
    out_rows, width = out_ref.shape
    r = lax.broadcasted_iota(jnp.int32, (out_rows, n), 0)
    source = lax.broadcasted_iota(jnp.int32, (out_rows, n), 1)
    quarter = lax.broadcasted_iota(jnp.int32, (out_rows, 1), 0) // 2 % 4
    core = (lax.axis_index("core") + dc) % 2
    pick = (source == (r // 8) * 4 + core * 2 + r % 2).astype(BF)
    picked = jnp.dot(pick, heads, preferred_element_type=F32).astype(BF)
    for k in range(0, width, 256):
        parts = [
            jnp.dot(
                picked,
                out_proj_ref[:, j * width + k : j * width + k + 256],
                preferred_element_type=F32,
            )
            for j in range(4)
        ]
        out_ref[:, k : k + 256] = pick_part(parts, 4, quarter).astype(out_ref.dtype)


def add_places(got_ref):
    acc = got_ref[0].astype(F32)
    for p in range(1, got_ref.shape[0]):
        acc = acc + got_ref[p].astype(F32)
    return acc


def gather_sum(got_ref, extra_ref, ids_ref, weights_ref, out_ref, held_ref):
    width = held_ref.shape[1]
    held_ref[...] = add_places(got_ref)
    first = (lax.axis_index("tensor") == 0).astype(F32)
    for j in range(4):
        columns = slice(j * width, (j + 1) * width)
        term = first * extra_ref[:, columns].astype(F32)
        out_ref[:, columns] = (held_ref[2 * j : 2 * j + 2] + term).astype(BF)
    ids, weights = ids_ref[...], weights_ref[...].astype(F32)
    lane = lax.broadcasted_iota(jnp.int32, (ids.shape[0], 128), 1)
    table = jnp.zeros(lane.shape, F32)
    for k in range(ids.shape[1]):
        table = table + jnp.where(lane == ids[:, k : k + 1], weights[:, k : k + 1], 0.0)
    out_ref[:, 4 * width :] = table.astype(BF)


def add_pair(here_ref, there_ref, out_ref):
    width = here_ref.shape[1] - 128
    both = here_ref[:, :width].astype(F32) + there_ref[:, :width].astype(F32)
    out_ref[:, :width] = both.astype(BF)
    out_ref[:, width:] = here_ref[:, width:]


def normalise(a_ref, b_ref, c_ref, d_ref, gain_ref, attended_ref, out_ref, held_ref):
    width = attended_ref.shape[1]
    half = width // 2
    gain = gain_ref[...].astype(F32).reshape(1, width)
    for role, (here_ref, there_ref) in enumerate(((a_ref, b_ref), (c_ref, d_ref))):
        acc = here_ref[:, :width].astype(F32) + there_ref[:, :width].astype(F32)
        if role == 0:
            attended_ref[...] = acc
        mean_square = jnp.mean(acc * acc, axis=1, keepdims=True)
        normed = acc * lax.rsqrt(mean_square + 1e-06) * gain
        table = here_ref[:, width:].astype(F32)
        for h in range(2):
            at = 4 * h + 2 * role
            held_ref[at : at + 2, :half] = normed[:, h * half : (h + 1) * half]
            held_ref[at : at + 2, half:] = table
    block = held_ref[...].astype(BF)
    for p in range(out_ref.shape[0]):
        out_ref[p] = block


def spread_sum(got_ref, out_ref, held_ref):
    half = held_ref.shape[1]
    held_ref[...] = add_places(got_ref)
    first = lax.axis_index("role") == 0
    for h in range(2):
        columns = slice(h * half, (h + 1) * half)
        own = held_ref[4 * h : 4 * h + 2]
        other = held_ref[4 * h + 2 : 4 * h + 4]
        low = jnp.where(first, own, other).astype(BF)
        high = jnp.where(first, other, own).astype(BF)
        for t in range(4):
            out_ref[t, :, columns] = low
            out_ref[4 + t, :, columns] = high


def which_half(rows):
    return lax.broadcasted_iota(jnp.int32, (rows, 1), 0) // 4 % 2


def hidden(rows_ref, gate_ref, up_ref):
    n, step = rows_ref.shape[0], 512
    width = gate_ref.shape[1] // 2
    half = which_half(n)

    units = gate_ref.shape[2]
    sums = [jnp.zeros((n, 2 * units), F32) for _ in range(2)]
    for k in range(0, width, step):
        rows = rows_ref[:, k : k + step]
        for h in range(2):
            at = slice(h * width + k, h * width + k + step)
            weights = jnp.concatenate([gate_ref[0, at], up_ref[0, at]], axis=1)
            sums[h] = sums[h] + jnp.dot(rows, weights, preferred_element_type=F32)
    value = pick_part(sums, 2, half)
    other = jnp.where(half == 0, pltpu.roll(value, n - 4, 0), pltpu.roll(value, 4, 0))
    value = value + other
    gate, upper = value[:, :units], value[:, units:]
    lane = lax.broadcasted_iota(jnp.int32, (n, 128), 1)
    chosen = jnp.where(lane == lax.axis_index(("y", "x", "core")), rows_ref[:, width:].astype(F32), 0.0)
    coef = jnp.sum(chosen, axis=1, keepdims=True)
    act = (gate / (1.0 + jnp.exp(-gate)) * upper).astype(BF)
    return act, coef


def fall(act, coef, down_ref, out_ref):
    width, step = out_ref.shape[1], 512
    half = which_half(act.shape[0])
    for at in range(0, width, step):
        parts = [
            jnp.dot(act, down_ref[0, :, k : k + step], preferred_element_type=F32)
            for k in (at, width + at)
        ]
        out_ref[:, at : at + step] = (coef * pick_part(parts, 2, half)).astype(out_ref.dtype)


def activate(rows_ref, gate_ref, up_ref, act_ref, coef_ref):
    act, coef = hidden(rows_ref, gate_ref, up_ref)
    act_ref[...] = act
    coef_ref[...] = jnp.broadcast_to(coef, coef_ref.shape)


def through(rows_ref, gate_ref, up_ref, down_ref, out_ref):
    act, coef = hidden(rows_ref, gate_ref, up_ref)
    fall(act, coef, down_ref, out_ref)


def descend(act_ref, coef_ref, down_ref, out_ref):
    fall(act_ref[...], coef_ref[:, :1], down_ref, out_ref)


SCALAR = pl.BlockSpec(memory_space=pltpu.SMEM)
WHOLE = pl.BlockSpec(memory_space=pltpu.VMEM)


def kernel(body, shapes, inputs, specs=None, scratch=(), work=(0, 0), mib=12):
    return pl.pallas_call(
        body,
        out_shape=shapes,
        in_specs=specs or [WHOLE] * len(inputs),
        out_specs=jax.tree.map(lambda _: WHOLE, shapes),
        scratch_shapes=list(scratch),
        compiler_params=pltpu.CompilerParams(vmem_limit_bytes=mib * 1024 * 1024),
        cost_estimate=pl.CostEstimate(flops=work[0], bytes_accessed=work[1], transcendentals=0),
    )(*inputs)


def shards(
    request_latent_cache,
    queries,
    cache_lengths,
    residual_in,
    value_up_weight,
    out_proj,
    norm_gain,
    gate_proj,
    up_proj,
    down_proj,
    expert_ids,
    route_weights,
):
    local_requests = request_latent_cache.shape[0]
    latent = value_up_weight.shape[1]
    experts, width = 32, residual_in.shape[1]

    slots, depth = request_latent_cache.shape[1:]
    n_heads = queries.shape[1]
    parts = pl.pallas_call(
        attend,
        grid=(local_requests,),
        out_shape=[pltpu.VMEM((local_requests, experts, latent + 128), BF)] * 4,
        in_specs=[
            SCALAR,
            pl.BlockSpec((1, depth, n_heads), lambda r: (r, 0, 0)),
            pl.BlockSpec((1, depth, slots // 2), lambda r: (r, 0, 0)),
            pl.BlockSpec((1, depth, slots // 2), lambda r: (r, 0, 1)),
        ],
        out_specs=[pl.BlockSpec((1, experts, latent + 128), lambda r: (r, 0, 0))] * 4,
        compiler_params=pltpu.CompilerParams(vmem_limit_bytes=58 * 1024 * 1024),
    )(
        cache_lengths,
        jnp.swapaxes(queries, 1, 2),
        jnp.swapaxes(request_latent_cache, 1, 2),
        jnp.swapaxes(request_latent_cache, 1, 2),
    )
    parts = [parts[0]] + [
        lax.ppermute(parts[s], "tensor", [(i, (i + s) % 4) for i in range(4)]) for s in (1, 2, 3)
    ]
    context = kernel(
        combine, jax.ShapeDtypeStruct((experts, local_requests, latent), BF), parts
    )
    rows = trade(context, PLANE + ("core",))
    rows = rows.reshape(experts * local_requests, latent)
    shape = jax.ShapeDtypeStruct
    places, packed = 16, 4 * local_requests
    quarter, middle = width // 4, width // 2
    away, acc = [
        kernel(
            functools.partial(project, dc),
            shape((places * packed, quarter), kind),
            [rows, value_up_weight, out_proj],
            work=(2 * places * packed * 128 * width, 2 * 128 * width),
        )
        for dc, kind in ((1, BF), (0, F32))
    ]
    acc = (acc + other_core(away).astype(F32)).astype(BF)
    acc = trade(acc.reshape(places, packed, quarter), PLANE)
    routed_width = width + 128
    block = kernel(
        gather_sum,
        shape((local_requests, routed_width), BF),
        [acc, residual_in, expert_ids, route_weights],
        scratch=[pltpu.VMEM((packed, quarter), F32)],
    )
    block = kernel(
        add_pair, shape((local_requests, routed_width), BF), [block, along(block, 1)]
    )
    far, near, mate = along(block, 5), along(block, 6), along(block, 2)
    attended, block = kernel(
        normalise,
        (
            shape((local_requests, width), F32),
            shape((places, packed, middle + 128), BF),
        ),
        [block, mate, near, far, norm_gain],
        scratch=[pltpu.VMEM((packed, middle + 128), F32)],
    )
    block = trade(block, PLANE).reshape(places * packed, middle + 128)
    across = other_core(block)

    n_rows, units = block.shape[0], gate_proj.shape[2]
    flops, size = 2 * n_rows * width * units, 2 * width * units
    act, coef = kernel(
        activate,
        (shape((n_rows, units), BF), shape((n_rows, 128), F32)),
        [block, gate_proj, up_proj],
        work=(2 * flops, 2 * size),
    )
    across, act, coef = lax.optimization_barrier((across, act, coef))
    sent = kernel(
        through,
        shape((n_rows, middle), BF),
        [across, gate_proj, up_proj, down_proj],
        work=(3 * flops, 3 * size),
    )
    sent = other_core(sent)
    acc = kernel(
        descend,
        shape((n_rows, middle), F32),
        [act, coef, down_proj],
        work=(flops, size),
    )
    acc = (acc + sent.astype(F32)).astype(BF)
    acc = trade(acc.reshape(places, packed, middle), PLANE)
    acc = kernel(
        spread_sum,
        shape((8, local_requests, width), BF),
        [acc],
        scratch=[pltpu.VMEM((packed, middle), F32)],
    )
    acc = trade(acc, LINE)
    routed = jnp.sum(acc.astype(F32), axis=0)
    return (attended, routed)


def solution(mesh):
    sizes = (mesh.shape["role"], SIDE, SIDE, 2, mesh.shape["tensor"])
    names = ("role", "y", "x", "core", "tensor")
    expert = ("y", "x", "core")
    own = ("role",) + expert
    placed = (
        P(own, "tensor", None),
        P(own, None, None),
        P(own),
        P(own, None),
        P(expert + ("tensor",), None, None),
        P(expert + ("tensor",), None),
        P(),
        P(expert, None, ("role", "tensor")),
        P(expert, None, ("role", "tensor")),
        P(expert, ("role", "tensor"), None),
        P(own, None),
        P(own, None),
    )
    return jax.shard_map(
        shards,
        mesh=jax.sharding.Mesh(mesh.devices.reshape(sizes), names),
        in_specs=placed,
        out_specs=(P(own, None), P(own, None)),
        check_vma=False,
    )
```

```python
import functools

import jax
import jax.numpy as jnp
from jax import lax
from jax.experimental import pallas as pl
from jax.experimental.pallas import tpu as pltpu
from jax.sharding import PartitionSpec as P

SCORE_SCALE = 192.0 ** (-0.5)
SIDE = 4
BF = jnp.bfloat16
F32 = jnp.float32


PLANE = ("x", "y")
LINE = ("role", "tensor")


def other_core(value):
    return lax.ppermute(value, "core", [(0, 1), (1, 0)])


def along(value, bits):
    return lax.ppermute(value, LINE, [(i, i ^ bits) for i in range(8)])


def trade(value, axes):
    return lax.all_to_all(value, axes, 0, 0, tiled=True)


def in_three(value):
    high = value.astype(BF).astype(F32)
    rest = value - high
    middle = rest.astype(BF).astype(F32)
    return high, middle, rest - middle


def attend(length_ref, q_ref, first_ref, last_ref, *out_refs):
    heads, half = q_ref.shape[2], first_ref.shape[2]
    slots = 2 * half
    latent = out_refs[0].shape[2] - 128
    experts = out_refs[0].shape[1]
    row = lax.broadcasted_iota(jnp.int32, (heads, heads), 0)
    column = lax.broadcasted_iota(jnp.int32, (heads, heads), 1)
    owner = (lax.axis_index("tensor") + row // experts) % 4
    place = row % experts
    expert = (place // 2 % SIDE * SIDE + place // (2 * SIDE)) * 2 + place % 2
    pick = (column == expert * 4 + owner).astype(BF)
    q = lax.dot_general(pick, q_ref[0], (((1,), (1,)), ((), ())), preferred_element_type=F32)
    q = q.astype(BF)
    logits = [
        jnp.dot(q, keys_ref[0], preferred_element_type=F32) for keys_ref in (first_ref, last_ref)
    ]
    logits = jnp.concatenate(logits, axis=1) * SCORE_SCALE
    position = lax.axis_index("tensor") * slots + lax.broadcasted_iota(jnp.int32, (1, slots), 1)
    live = position < length_ref[pl.program_id(0)]
    masked = jnp.where(live, logits, -1e30)
    top = jnp.max(masked, axis=1, keepdims=True)
    expo = jnp.where(live, jnp.exp(masked - top), 0.0)
    total = jnp.sum(expo, axis=1, keepdims=True)
    expo = expo.astype(BF)
    numer = jnp.zeros((heads, latent), F32)
    for part, keys_ref in ((expo[:, :half], first_ref), (expo[:, half:], last_ref)):
        numer = numer + lax.dot_general(
            part, keys_ref[0, :latent], (((1,), (1,)), ((), ())), preferred_element_type=F32
        )
    part = (numer / jnp.maximum(total, 1.0)).astype(BF)
    for t, out_ref in enumerate(out_refs):
        out_ref[0, :, :latent] = part[t * experts : (t + 1) * experts]
    lane = lax.broadcasted_iota(jnp.int32, (heads, 128), 1)
    stats = jnp.zeros((heads, 128), F32)
    for i, column in enumerate((*in_three(top), *in_three(total))):
        stats = jnp.where(lane == i, column, stats)
    stats = stats.astype(BF)
    for t, out_ref in enumerate(out_refs):
        out_ref[0, :, latent:] = stats[t * experts : (t + 1) * experts]


def combine(*refs):
    parts_refs, out_ref = refs[:-1], refs[-1]
    experts, requests, latent = out_ref.shape
    contexts = []
    for r in range(requests):
        tops, totals = [], []
        for t in range(4):
            s = parts_refs[t][r, :, latent:].astype(F32)
            tops.append(s[:, 0:1] + s[:, 1:2] + s[:, 2:3])
            totals.append(s[:, 3:4] + s[:, 4:5] + s[:, 5:6])
        top = jnp.maximum(jnp.maximum(tops[0], tops[1]), jnp.maximum(tops[2], tops[3]))
        weights = [jnp.exp(a - top) * b for a, b in zip(tops, totals)]
        whole = weights[0] + weights[1] + weights[2] + weights[3]
        acc = jnp.zeros((experts, latent), F32)
        for t in range(4):
            acc = acc + (weights[t] / whole) * parts_refs[t][r, :, :latent].astype(F32)
        contexts.append(acc)
    out_ref[...] = jnp.stack(contexts, axis=1).astype(BF)


def pick_part(parts, count, part):
    value = parts[0]
    for j in range(1, count):
        value = jnp.where(part == j, parts[j], value)
    return value


def project(dc, rows_ref, value_ref, out_proj_ref, out_ref):
    n = rows_ref.shape[0]
    heads = jnp.dot(rows_ref[...], value_ref[0], preferred_element_type=F32).astype(BF)
    out_rows, width = out_ref.shape
    r = lax.broadcasted_iota(jnp.int32, (out_rows, n), 0)
    source = lax.broadcasted_iota(jnp.int32, (out_rows, n), 1)
    quarter = lax.broadcasted_iota(jnp.int32, (out_rows, 1), 0) // 2 % 4
    core = (lax.axis_index("core") + dc) % 2
    pick = (source == (r // 8) * 4 + core * 2 + r % 2).astype(BF)
    picked = jnp.dot(pick, heads, preferred_element_type=F32).astype(BF)
    for k in range(0, width, 256):
        parts = [
            jnp.dot(
                picked,
                out_proj_ref[:, j * width + k : j * width + k + 256],
                preferred_element_type=F32,
            )
            for j in range(4)
        ]
        out_ref[:, k : k + 256] = pick_part(parts, 4, quarter).astype(out_ref.dtype)


def add_places(got_ref):
    acc = got_ref[0].astype(F32)
    for p in range(1, got_ref.shape[0]):
        acc = acc + got_ref[p].astype(F32)
    return acc


def gather_sum(got_ref, extra_ref, ids_ref, weights_ref, out_ref, held_ref):
    width = held_ref.shape[1]
    held_ref[...] = add_places(got_ref)
    first = (lax.axis_index("tensor") == 0).astype(F32)
    for j in range(4):
        columns = slice(j * width, (j + 1) * width)
        term = first * extra_ref[:, columns].astype(F32)
        out_ref[:, columns] = (held_ref[2 * j : 2 * j + 2] + term).astype(BF)
    ids, weights = ids_ref[...], weights_ref[...].astype(F32)
    lane = lax.broadcasted_iota(jnp.int32, (ids.shape[0], 128), 1)
    table = jnp.zeros(lane.shape, F32)
    for k in range(ids.shape[1]):
        table = table + jnp.where(lane == ids[:, k : k + 1], weights[:, k : k + 1], 0.0)
    out_ref[:, 4 * width :] = table.astype(BF)


def add_pair(here_ref, there_ref, out_ref):
    width = here_ref.shape[1] - 128
    both = here_ref[:, :width].astype(F32) + there_ref[:, :width].astype(F32)
    out_ref[:, :width] = both.astype(BF)
    out_ref[:, width:] = here_ref[:, width:]


def normalise(a_ref, b_ref, c_ref, d_ref, gain_ref, attended_ref, out_ref, held_ref):
    width = attended_ref.shape[1]
    half = width // 2
    gain = gain_ref[...].astype(F32).reshape(1, width)
    for role, (here_ref, there_ref) in enumerate(((a_ref, b_ref), (c_ref, d_ref))):
        acc = here_ref[:, :width].astype(F32) + there_ref[:, :width].astype(F32)
        if role == 0:
            attended_ref[...] = acc
        mean_square = jnp.mean(acc * acc, axis=1, keepdims=True)
        normed = acc * lax.rsqrt(mean_square + 1e-06) * gain
        table = here_ref[:, width:].astype(F32)
        for h in range(2):
            at = 4 * h + 2 * role
            held_ref[at : at + 2, :half] = normed[:, h * half : (h + 1) * half]
            held_ref[at : at + 2, half:] = table
    block = held_ref[...].astype(BF)
    for p in range(out_ref.shape[0]):
        out_ref[p] = block


def spread_sum(got_ref, out_ref, held_ref):
    half = held_ref.shape[1]
    held_ref[...] = add_places(got_ref)
    first = lax.axis_index("role") == 0
    for h in range(2):
        columns = slice(h * half, (h + 1) * half)
        own = held_ref[4 * h : 4 * h + 2]
        other = held_ref[4 * h + 2 : 4 * h + 4]
        low = jnp.where(first, own, other).astype(BF)
        high = jnp.where(first, other, own).astype(BF)
        for t in range(4):
            out_ref[t, :, columns] = low
            out_ref[4 + t, :, columns] = high


def line_sum(got_ref, out_ref):
    out_ref[...] = add_places(got_ref)


def which_half(rows):
    return lax.broadcasted_iota(jnp.int32, (rows, 1), 0) // 4 % 2


def hidden(rows_ref, gate_ref, up_ref):
    n, step = rows_ref.shape[0], 512
    width = gate_ref.shape[1] // 2
    half = which_half(n)

    units = gate_ref.shape[2]
    sums = [jnp.zeros((n, 2 * units), F32) for _ in range(2)]
    for k in range(0, width, step):
        rows = rows_ref[:, k : k + step]
        for h in range(2):
            at = slice(h * width + k, h * width + k + step)
            weights = jnp.concatenate([gate_ref[0, at], up_ref[0, at]], axis=1)
            sums[h] = sums[h] + jnp.dot(rows, weights, preferred_element_type=F32)
    value = pick_part(sums, 2, half)
    other = jnp.where(half == 0, pltpu.roll(value, n - 4, 0), pltpu.roll(value, 4, 0))
    value = value + other
    gate, upper = value[:, :units], value[:, units:]
    lane = lax.broadcasted_iota(jnp.int32, (n, 128), 1)
    chosen = jnp.where(lane == lax.axis_index(("y", "x", "core")), rows_ref[:, width:].astype(F32), 0.0)
    coef = jnp.sum(chosen, axis=1, keepdims=True)
    act = (gate / (1.0 + jnp.exp(-gate)) * upper).astype(BF)
    return act, coef


def fall(act, coef, down_ref, out_ref):
    width, step = out_ref.shape[1], 512
    half = which_half(act.shape[0])
    for at in range(0, width, step):
        parts = [
            jnp.dot(act, down_ref[0, :, k : k + step], preferred_element_type=F32)
            for k in (at, width + at)
        ]
        out_ref[:, at : at + step] = (coef * pick_part(parts, 2, half)).astype(out_ref.dtype)


def activate(rows_ref, gate_ref, up_ref, act_ref, coef_ref):
    act, coef = hidden(rows_ref, gate_ref, up_ref)
    act_ref[...] = act
    coef_ref[...] = jnp.broadcast_to(coef, coef_ref.shape)


def through(rows_ref, gate_ref, up_ref, down_ref, out_ref):
    act, coef = hidden(rows_ref, gate_ref, up_ref)
    fall(act, coef, down_ref, out_ref)


def descend(act_ref, coef_ref, down_ref, out_ref):
    fall(act_ref[...], coef_ref[:, :1], down_ref, out_ref)


SCALAR = pl.BlockSpec(memory_space=pltpu.SMEM)
WHOLE = pl.BlockSpec(memory_space=pltpu.VMEM)


def kernel(body, shapes, inputs, specs=None, scratch=(), work=(0, 0), mib=12):
    return pl.pallas_call(
        body,
        out_shape=shapes,
        in_specs=specs or [WHOLE] * len(inputs),
        out_specs=jax.tree.map(lambda _: WHOLE, shapes),
        scratch_shapes=list(scratch),
        compiler_params=pltpu.CompilerParams(vmem_limit_bytes=mib * 1024 * 1024),
        cost_estimate=pl.CostEstimate(flops=work[0], bytes_accessed=work[1], transcendentals=0),
    )(*inputs)


def shards(
    request_latent_cache,
    queries,
    cache_lengths,
    residual_in,
    value_up_weight,
    out_proj,
    norm_gain,
    gate_proj,
    up_proj,
    down_proj,
    expert_ids,
    route_weights,
):
    local_requests = request_latent_cache.shape[0]
    latent = value_up_weight.shape[1]
    experts, width = 32, residual_in.shape[1]

    slots, depth = request_latent_cache.shape[1:]
    n_heads = queries.shape[1]
    parts = pl.pallas_call(
        attend,
        grid=(local_requests,),
        out_shape=[pltpu.VMEM((local_requests, experts, latent + 128), BF)] * 4,
        in_specs=[
            SCALAR,
            pl.BlockSpec((1, depth, n_heads), lambda r: (r, 0, 0)),
            pl.BlockSpec((1, depth, slots // 2), lambda r: (r, 0, 0)),
            pl.BlockSpec((1, depth, slots // 2), lambda r: (r, 0, 1)),
        ],
        out_specs=[pl.BlockSpec((1, experts, latent + 128), lambda r: (r, 0, 0))] * 4,
        compiler_params=pltpu.CompilerParams(vmem_limit_bytes=58 * 1024 * 1024),
    )(
        cache_lengths,
        jnp.swapaxes(queries, 1, 2),
        jnp.swapaxes(request_latent_cache, 1, 2),
        jnp.swapaxes(request_latent_cache, 1, 2),
    )
    parts = [parts[0]] + [
        lax.ppermute(parts[s], "tensor", [(i, (i + s) % 4) for i in range(4)]) for s in (1, 2, 3)
    ]
    context = kernel(
        combine, jax.ShapeDtypeStruct((experts, local_requests, latent), BF), parts
    )
    rows = trade(context, PLANE + ("core",))
    rows = rows.reshape(experts * local_requests, latent)
    shape = jax.ShapeDtypeStruct
    places, packed = 16, 4 * local_requests
    quarter, middle = width // 4, width // 2
    away, acc = [
        kernel(
            functools.partial(project, dc),
            shape((places * packed, quarter), kind),
            [rows, value_up_weight, out_proj],
            work=(2 * places * packed * 128 * width, 2 * 128 * width),
        )
        for dc, kind in ((1, BF), (0, F32))
    ]
    acc = (acc + other_core(away).astype(F32)).astype(BF)
    acc = trade(acc.reshape(places, packed, quarter), PLANE)
    routed_width = width + 128
    block = kernel(
        gather_sum,
        shape((local_requests, routed_width), BF),
        [acc, residual_in, expert_ids, route_weights],
        scratch=[pltpu.VMEM((packed, quarter), F32)],
    )
    block = kernel(
        add_pair, shape((local_requests, routed_width), BF), [block, along(block, 1)]
    )
    far, near, mate = along(block, 5), along(block, 6), along(block, 2)
    attended, block = kernel(
        normalise,
        (
            shape((local_requests, width), F32),
            shape((places, packed, middle + 128), BF),
        ),
        [block, mate, near, far, norm_gain],
        scratch=[pltpu.VMEM((packed, middle + 128), F32)],
    )
    block = trade(block, PLANE).reshape(places * packed, middle + 128)
    across = other_core(block)

    n_rows, units = block.shape[0], gate_proj.shape[2]
    flops, size = 2 * n_rows * width * units, 2 * width * units
    act, coef = kernel(
        activate,
        (shape((n_rows, units), BF), shape((n_rows, 128), F32)),
        [block, gate_proj, up_proj],
        work=(2 * flops, 2 * size),
    )
    across, act, coef = lax.optimization_barrier((across, act, coef))
    sent = kernel(
        through,
        shape((n_rows, middle), BF),
        [across, gate_proj, up_proj, down_proj],
        work=(3 * flops, 3 * size),
    )
    sent = other_core(sent)
    acc = kernel(
        descend,
        shape((n_rows, middle), F32),
        [act, coef, down_proj],
        work=(flops, size),
    )
    acc = (acc + sent.astype(F32)).astype(BF)
    acc = trade(acc.reshape(places, packed, middle), PLANE)
    acc = kernel(
        spread_sum,
        shape((8, local_requests, width), BF),
        [acc],
        scratch=[pltpu.VMEM((packed, middle), F32)],
    )
    acc = trade(acc, LINE)
    routed = kernel(line_sum, shape((local_requests, width), F32), [acc])
    return (attended, routed)


def solution(mesh):
    sizes = (mesh.shape["role"], SIDE, SIDE, 2, mesh.shape["tensor"])
    names = ("role", "y", "x", "core", "tensor")
    expert = ("y", "x", "core")
    own = ("role",) + expert
    placed = (
        P(own, "tensor", None),
        P(own, None, None),
        P(own),
        P(own, None),
        P(expert + ("tensor",), None, None),
        P(expert + ("tensor",), None),
        P(),
        P(expert, None, ("role", "tensor")),
        P(expert, None, ("role", "tensor")),
        P(expert, ("role", "tensor"), None),
        P(own, None),
        P(own, None),
    )
    return jax.shard_map(
        shards,
        mesh=jax.sharding.Mesh(mesh.devices.reshape(sizes), names),
        in_specs=placed,
        out_specs=(P(own, None), P(own, None)),
        check_vma=False,
    )
```
